32 devices in a mesh: page: 2 (over y), blk: 8 (over z, x), head: 2 (over core).
Axes of the slice: x: 2, y: 2, z: 4, core: 2. Of those that a mesh axis runs over, the one named last changes fastest.
Arguments:
- vis_tokens: bfloat16 [2, 1152, 768], P('page', 'blk'), may hold values from -6 to 6
- query_tokens: bfloat16 [2, 256, 768], P('page'), may hold values from -6 to 6
- answer_lengths: int32 [2], P('page'), may hold values from 5 to 256, as said below
- norm_gains: float32 [6, 768], replicated, may hold values from 0.1 to 1.9
- bias_table: float32 [12, 23, 23], P('head'), may hold values from -4 to 4
- window_qkv: bfloat16 [3, 768, 768], P(None, None, 'head'), may hold values from -0.3125 to 0.3125
- window_out: bfloat16 [768, 768], P('head'), may hold values from -0.21875 to 0.21875
- causal_qkv: bfloat16 [3, 768, 768], P(None, None, 'head'), may hold values from -0.3125 to 0.3125
- causal_out: bfloat16 [768, 768], P('head'), may hold values from -0.3125 to 0.3125
- read_qkv: bfloat16 [3, 768, 768], P(None, None, 'head'), may hold values from -0.3125 to 0.3125
- read_out: bfloat16 [768, 768], P('head'), may hold values from -0.875 to 0.875
- write_qkv: bfloat16 [3, 768, 768], P(None, None, 'head'), may hold values from -0.3125 to 0.3125
- write_out: bfloat16 [768, 768], P('head'), may hold values from -0.4375 to 0.4375
- vis_up: bfloat16 [768, 3072], P(None, 'head'), may hold values from -0.21875 to 0.21875
- vis_down: bfloat16 [3072, 768], P('head'), may hold values from -0.109375 to 0.109375
- query_up: bfloat16 [768, 3072], P(None, 'head'), may hold values from -0.21875 to 0.21875
- query_down: bfloat16 [3072, 768], P('head'), may hold values from -0.109375 to 0.109375
- cot_vis: bfloat16 [2, 1152, 768], P('page', 'blk'), may hold values from -6 to 6
- cot_query: bfloat16 [2, 256, 768], P('page'), may hold values from -6 to 6
Outputs:
- vis_out: bfloat16 [2, 1152, 768], P('page', 'blk')
- query_out: bfloat16 [2, 256, 768], P('page')
- grad_visual: float32 [2, 1152, 768], P('page', 'blk')
- grad_query: float32 [2, 256, 768], P('page')
- grad_gains: float32 [6, 768], P(None, ('page', 'blk'))
- grad_table: float32 [12, 23, 23], P('head')
- grad_window_qkv: float32 [3, 768, 768], P(None, ('page', 'blk'), 'head')
- grad_window_out: float32 [768, 768], P('head', ('page', 'blk'))
- grad_causal_qkv: float32 [3, 768, 768], P(None, ('page', 'blk'), 'head')
- grad_causal_out: float32 [768, 768], P('head', ('page', 'blk'))
- grad_read_qkv: float32 [3, 768, 768], P(None, ('page', 'blk'), 'head')
- grad_read_out: float32 [768, 768], P('head', ('page', 'blk'))
- grad_write_qkv: float32 [3, 768, 768], P(None, ('page', 'blk'), 'head')
- grad_write_out: float32 [768, 768], P('head', ('page', 'blk'))
- grad_vis_up: float32 [768, 3072], P(('page', 'blk'), 'head')
- grad_vis_down: float32 [3072, 768], P('head', ('page', 'blk'))
- grad_query_up: float32 [768, 3072], P(('page', 'blk'), 'head')
- grad_query_down: float32 [3072, 768], P('head', ('page', 'blk'))
The draws below stay inside these ranges and needn't reach their ends.
Inputs may be any that keep to these rules, and one draw needn't show every extreme that they name: `answer_lengths`: answer length of each page; some page has all 256 query tokens live.
All inputs are finite; a program needn't handle non-finite values.
Results may differ from the reference program's by a relative error of at most 0.035.
The reference program's roundings to bfloat16 on the way count: a program that leaves them out, or rounds other values in their place, can miss the bound.
Values may be sent and summed in bfloat16 or wider, within the bound.
A program may use at most 256 MiB of HBM per device.

```python
import jax
import jax.numpy as jnp
from jax import lax

D = 768
HEADS = 12
HEAD_DIM = 64
FF = 3072
WIN = 12
Q = 256
PAGES = 2
PATCHES = 1152


def draw_answer_lengths(key, part):
    key = jax.random.fold_in(key, 11)
    first_key, second_key = jax.random.split(key)
    drawn = jax.random.randint(first_key, (PAGES,), 5, Q + 1)
    longest = jax.random.randint(second_key, (), 0, PAGES)
    return jnp.where(jnp.arange(PAGES) == longest, Q, drawn).astype(jnp.int32)


def block_scale(key, dims, cuts, low, top_value):
    loudness, own = 1.0, jax.random.fold_in(key, 6)
    for axis_at, parts in cuts:
        steps = jnp.exp(jax.random.uniform(jax.random.fold_in(own, axis_at), (parts,), jnp.float32, low / len(cuts), top_value / len(cuts)))
        loudness = loudness * jnp.repeat(steps, dims[axis_at] // parts).reshape([-1 if axis == axis_at else 1 for axis in range(len(dims))])
    return loudness


def noise(own_key, dims, scale, bound, cuts=(), dtype=jnp.bfloat16):
    values = scale * jax.random.normal(own_key, dims, jnp.float32)
    if cuts:
        values = values * block_scale(own_key, dims, cuts, -0.22, 0.18)
    return jnp.clip(values, -bound, bound).astype(dtype)


def setup_inputs(seed: int = 0) -> dict:
    splits = jax.random.split(jax.random.key(seed), 20)
    vis_tokens = noise(splits[0], (PAGES, PATCHES, D), 1.0, 6.0, ((0, 2), (1, 8)))
    query_tokens = noise(splits[1], (PAGES, Q, D), 1.0, 6.0, ((0, 2),))
    answer_lengths = draw_answer_lengths(jax.random.fold_in(splits[19], 71), 0)
    norm_gains = jnp.clip(1.0 + 0.18 * jax.random.normal(splits[3], (6, D), jnp.float32), 0.1, 1.9)
    bias_table = noise(splits[4], (HEADS, 2 * WIN - 1, 2 * WIN - 1), 1.0, 4.0, ((0, 2),), jnp.float32)
    window_qkv = noise(splits[5], (3, D, D), (D // 2) ** -0.5, 0.3125, ((2, 2),))
    window_out = noise(splits[6], (D, D), D ** -0.5, 0.21875, ((0, 2),))
    causal_qkv = noise(splits[7], (3, D, D), (D // 2) ** -0.5, 0.3125, ((2, 2),))
    causal_out = noise(splits[8], (D, D), (D // 2) ** -0.5, 0.3125, ((0, 2),))
    read_qkv = noise(splits[9], (3, D, D), (D // 2) ** -0.5, 0.3125, ((2, 2),))
    read_out = noise(splits[10], (D, D), (D // 16) ** -0.5, 0.875, ((0, 2),))
    write_qkv = noise(splits[11], (3, D, D), (D // 2) ** -0.5, 0.3125, ((2, 2),))
    write_out = noise(splits[12], (D, D), (D // 4) ** -0.5, 0.4375, ((0, 2),))
    vis_up = noise(splits[13], (D, FF), D ** -0.5, 0.21875, ((1, 2),))
    vis_down = noise(splits[14], (FF, D), FF ** -0.5, 0.109375, ((0, 2),))
    query_up = noise(splits[15], (D, FF), D ** -0.5, 0.21875, ((1, 2),))
    query_down = noise(splits[16], (FF, D), FF ** -0.5, 0.109375, ((0, 2),))
    cot_vis = noise(splits[17], (PAGES, PATCHES, D), 1.0, 6.0, ((0, 2), (1, 8)))
    cot_query = noise(splits[18], (PAGES, Q, D), 1.0, 6.0, ((0, 2),))
    return dict(vis_tokens=vis_tokens, query_tokens=query_tokens, answer_lengths=answer_lengths, norm_gains=norm_gains, bias_table=bias_table, window_qkv=window_qkv, window_out=window_out, causal_qkv=causal_qkv, causal_out=causal_out, read_qkv=read_qkv, read_out=read_out, write_qkv=write_qkv, write_out=write_out, vis_up=vis_up, vis_down=vis_down, query_up=query_up, query_down=query_down, cot_vis=cot_vis, cot_query=cot_query)


HIGH = lax.Precision.HIGHEST

@jax.custom_vjp
def low(v):
    return lax.optimization_barrier(v.astype(jnp.bfloat16)).astype(jnp.float32)

@jax.custom_vjp
def low_back(v):
    return v

def low_keep(v):
    return (low(v), None)

def low_pass(kept, grad):
    return (grad,)

def back_keep(v):
    return (v, None)

def back_low(kept, grad):
    return (low(grad),)
low.defvjp(low_keep, low_pass)
low_back.defvjp(back_keep, back_low)

def low_both(tensor):
    return low_back(low(tensor))

def layer_norm(stream, gain):
    centred = stream - lax.optimization_barrier(jnp.mean(stream, axis=-1, keepdims=True))
    inverse = lax.rsqrt(lax.optimization_barrier(jnp.mean(centred * centred, axis=-1, keepdims=True)) + 1e-05)
    return centred * inverse * gain

def product(matrix, other):
    return jnp.dot(matrix, other, precision=HIGH)

def attention(queries, keyset, values, additive):
    scores = low_back(jnp.einsum('bqhe,bkhe->bhqk', queries, keyset, precision=HIGH) * HEAD_DIM ** (-0.5)) + additive
    soft_probs = jax.nn.softmax(scores, axis=-1)
    return jnp.einsum('bhqk,bkhe->bqhe', low(soft_probs), values, precision=HIGH)

def wide_attention(queries, keyset, values, additive):

    def head_fn(pieces):
        return attention(pieces[0][None, :, None], pieces[1][None, :, None], pieces[2][None, :, None], additive)[0, :, 0]
    stacked = lax.map(jax.checkpoint(head_fn), (queries.transpose(1, 0, 2), keyset.transpose(1, 0, 2), values.transpose(1, 0, 2)))
    return stacked.transpose(1, 0, 2)

def feed(stream, gain, up_weight, down_weight):
    normed = low(layer_norm(stream, gain))
    hidden = low_back(product(normed, up_weight))
    return low_back(product(low(jax.nn.gelu(hidden, approximate=False)), down_weight))

def page_forward(params, visual, query_in, length):
    norm_gains, bias_table, window_qkv, window_out, causal_qkv, causal_out, read_qkv, read_out, write_qkv, write_out, vis_up, vis_down, query_up, query_down = params
    patches = visual.shape[0]
    query_rows = query_in.shape[0]
    win_area = WIN * WIN
    windows = patches // win_area
    offsets = jnp.arange(WIN)
    one_hot = ((offsets[:, None] - offsets[None, :] + WIN - 1)[:, :, None] == jnp.arange(2 * WIN - 1)[None, None, :]).astype(jnp.float32)
    rel_bias = jnp.einsum('pqa,rsb,hab->hprqs', one_hot, one_hot, bias_table, precision=HIGH).reshape(HEADS, win_area, win_area)
    positions = jnp.arange(query_rows)
    causal_extra = jnp.where((positions[None, :] <= positions[:, None]) & (positions[None, :] < length), 0.0, -jnp.inf)
    write_extra = jnp.where(positions < length, 0.0, -jnp.inf)[None, :]

    def project(normed, weight):
        return low_both(product(normed, weight))
    win_norm = low(layer_norm(visual, norm_gains[0]))
    win_heads = [project(win_norm, window_qkv[member]).reshape(windows, win_area, HEADS, HEAD_DIM) for member in range(3)]
    win_mix = attention(win_heads[0], win_heads[1], win_heads[2], rel_bias[None]).reshape(patches, D)
    vis_one = visual + low_back(product(low_both(win_mix), window_out))
    causal_norm = low(layer_norm(query_in, norm_gains[1]))
    causal_heads = [project(causal_norm, causal_qkv[member]).reshape(1, query_rows, HEADS, HEAD_DIM) for member in range(3)]
    causal_mix = attention(causal_heads[0], causal_heads[1], causal_heads[2], causal_extra[None, None]).reshape(query_rows, D)
    query_one = query_in + low_back(product(low_both(causal_mix), causal_out))
    cross_query = low(layer_norm(query_one, norm_gains[2]))
    cross_vis = low(layer_norm(vis_one, norm_gains[3]))

    def heads_of(tensor):
        return tensor.reshape(tensor.shape[0], HEADS, HEAD_DIM)
    read_mix = wide_attention(heads_of(project(cross_query, read_qkv[0])), heads_of(project(cross_vis, read_qkv[1])), heads_of(project(cross_vis, read_qkv[2])), 0.0).reshape(query_rows, D)
    write_mix = wide_attention(heads_of(project(cross_vis, write_qkv[0])), heads_of(project(cross_query, write_qkv[1])), heads_of(project(cross_query, write_qkv[2])), write_extra).reshape(patches, D)
    query_two = query_one + low_back(product(low_both(read_mix), read_out))
    vis_two = vis_one + low_back(product(low_both(write_mix), write_out))
    vis_three = vis_two + feed(vis_two, norm_gains[4], vis_up, vis_down)
    query_three = query_two + feed(query_two, norm_gains[5], query_up, query_down)
    return (vis_three, query_three)

def reference(vis_tokens, query_tokens, answer_lengths, norm_gains, bias_table, window_qkv, window_out, causal_qkv, causal_out, read_qkv, read_out, write_qkv, write_out, vis_up, vis_down, query_up, query_down, cot_vis, cot_query):
    params = tuple((member.astype(jnp.float32) for member in (norm_gains, bias_table, window_qkv, window_out, causal_qkv, causal_out, read_qkv, read_out, write_qkv, write_out, vis_up, vis_down, query_up, query_down)))

    def forward(visual, query_in, weights):
        return jax.vmap(page_forward, in_axes=(None, 0, 0, 0))(weights, visual, query_in, answer_lengths)
    outputs, pullback = jax.vjp(forward, vis_tokens.astype(jnp.float32), query_tokens.astype(jnp.float32), params)
    grad_visual, grad_query, grads = pullback((cot_vis.astype(jnp.float32), cot_query.astype(jnp.float32)))
    return (outputs[0].astype(jnp.bfloat16), outputs[1].astype(jnp.bfloat16), grad_visual, grad_query, grads[0], grads[1], grads[2], grads[3], grads[4], grads[5], grads[6], grads[7], grads[8], grads[9], grads[10], grads[11], grads[12], grads[13])
```

```python
from functools import partial

import jax
import jax.numpy as jnp
from jax import lax
from jax.experimental import pallas as pl
from jax.experimental.pallas import tpu as pltpu
from jax.sharding import PartitionSpec as P

HEAD_DIM = 64
WIN = 12


EPS = 1e-05
HIGH = lax.Precision.HIGHEST
exact_gelu = partial(jax.nn.gelu, approximate=False)

MESH = pl.DeviceIdType.MESH
BF = jnp.bfloat16
F32 = jnp.float32
DIFFS = 2 * WIN - 1
AREA = WIN * WIN
TABLE_LANES = 640
STRIP_LANES = 384


def mm(a, b):
    return jnp.dot(a, b, preferred_element_type=F32)


def mm_nt(a, b, precision=None):
    return lax.dot_general(a, b, (((1,), (1,)), ((), ())), precision=precision, preferred_element_type=F32)


def mm_tn(a, b):
    return lax.dot_general(a, b, (((0,), (0,)), ((), ())), preferred_element_type=F32)


def iota(shape, axis):
    return lax.broadcasted_iota(jnp.int32, shape, axis)


def loop(count, body, unroll=1):
    def step(i, carry):
        body(i)
        return carry

    lax.fori_loop(0, count, step, 0, unroll=unroll)


def row_loop(count, step, body):
    loop(count // step, lambda i: body(pl.ds(pl.multiple_of(i * step, step), step)))


def row_sum(count, step, width, body):
    def add(i, total):
        value = body(pl.ds(pl.multiple_of(i * step, step), step))
        return total + value.reshape(step // 8, 8, width).sum(0)

    total = lax.fori_loop(0, count // step, add, jnp.zeros((8, width), F32))
    return jnp.sum(total, axis=0, keepdims=True)


class Names:
    def __init__(self, **entries):
        self.__dict__.update(entries)


def scratch_shapes(R, Q, D, H, F, nb, own, cut):
    heads = H // HEAD_DIM
    nz = nb // 2
    half = D // 2
    B, S = BF, F32
    return dict(
        w_win=((3, D, H), B), w_win_out=((H, D), B), w_cau=((3, D, H), B), w_cau_out=((H, D), B),
        w_read=((3, D, H), B), w_read_out=((H, D), B), w_write=((3, D, H), B), w_write_out=((H, D), B),
        w_up=((D, F), B), w_down=((F, D), B),
        win_low=((R, D), B), win_inv=((R, 128), S), cau_low=((Q, D), B), cau_inv=((Q, 128), S),
        cq_low=((Q, D), B), cq_hat=((Q, D), S), cq_inv=((Q, 128), S),
        cv_low=((R, D), B), cv_hat=((R, D), S), cv_inv=((R, 128), S),
        fv_low=((R, D), B), fv_hat=((R, D), S), fv_inv=((R, 128), S),
        fq_low=((Q, D), B), fq_hat=((Q, D), S), fq_inv=((Q, 128), S),
        vis1=((R, D), S), vis2=((R, D), S), que1=((Q, D), S), que2=((Q, D), S),
        gvis2_low=((R, D), B), gvis1_low=((R, D), B), gque2_low=((Q, D), B), gque1_low=((Q, D), B),
        win_qkv=((3, R, H), B), cau_qkv=((3, Q, H), B),
        read_q=((Q, H), B), read_kv=((2, R, H), B), write_q=((R, H), B), write_kv=((2, Q, H), B),
        win_p=((heads, R, R), S), cau_p=((heads, Q, Q), S), read_p=((heads, Q, R), S), write_p=((heads, R, Q), S),
        da_v=((R, H), B), da_q=((Q, H), B),
        bias=((heads, R, R), S), strip=((heads, 16, STRIP_LANES), S), rolled=((heads, 16, TABLE_LANES), S),
        hot=((STRIP_LANES, TABLE_LANES), B),
        a_q=((Q, D), S), a_q_in=((Q, D), S), a_v=((R, D), S), a_v_in=((R, D), S),
        b_q=((Q, D), S), b_q_in=((Q, D), S), b_v=((R, D), S), b_v_in=((R, D), S),
        part=((Q, H + 128), S), part_in=((nb - 1, own, H + 128), S), mix=((Q, H + 128), S),
        read_att=((Q, H), B), cau_att=((Q, H), B),
        qg=((Q, 3 * H), S), qg_in=((nb - 1, own, 3 * H), S), qg_low=((Q, 3 * H), B),
        cau_g=((Q, 3 * H), B),
        dyq=((Q, 2 * F), B),
        dyf=((R, 2 * F), B), dyf_in=((R, 2 * F), B), dyc=((R, 4 * H), B), dyc_in=((R, 4 * H), B),
        dyw=((R, 4 * H), B), dyw_in=((R, 4 * H), B),
        sel=((2, half, D), B), sel_q=((2 * cut, D), B),
        xf=((2, half, R), B), xf_in=((2, half, R), B), xc=((2, half, R), B), xc_in=((2, half, R), B),
        xw=((2, half, R), B), xw_in=((2, half, R), B), x_out=((2, half, R), B),
        gf_in=((2 * F // D, half // 2, D), B), zf_in=((nz - 1, cut, 2 * F), B),
        gc_in=((4 * H // D, half // 2, D), B), zc_in=((nz - 1, cut, 4 * H), B),
        gw_in=((4 * H // D, half // 2, D), B), zw_in=((nz - 1, cut, 4 * H), B),
        tf=((cut, 2 * F), B), tf_in=((cut, 2 * F), B), tc=((cut, 4 * H), B), tc_in=((cut, 4 * H), B),
        tw=((cut, 4 * H), B), tw_in=((cut, 4 * H), B),
        gain=((8, D), S), gain_in=((8, D), S), gain_page=((8, D), S), gain_blk=((nb - 1, 8, D), S),
        tab=((8, TABLE_LANES), S), tab_in=((8, TABLE_LANES), S), tab_page=((8, TABLE_LANES), S),
        tab_blk=((nb - 1, 8, TABLE_LANES), S),
        slab_v=((cut, 2 * F + 8 * H), S), slab_q=((cut, 2 * F + 8 * H), S),
    )


WEIGHTS = ("w_win", "w_win_out", "w_cau", "w_cau_out", "w_read", "w_read_out", "w_write", "w_write_out", "w_vup", "w_vdown", "w_qup", "w_qdown")
LOAD_ORDER = ("w_cau", "w_cau_out", "w_win", "w_win_out", "w_read", "w_write", "w_write_out", "w_read_out", "w_vdown", "w_vup")
FEED_REFS = dict(w_vup="w_up", w_qup="w_up", w_vdown="w_down", w_qdown="w_down")


def block_kernel(
    names, nb, vis_ref, query_ref, length_ref, gains_ref, table_ref, cotv_ref, cotq_ref, *rest
):
    hbm = dict(zip(WEIGHTS, rest[:12]))
    vis_out, query_out, grad_vis, grad_query, gain_out, table_out, out_v, out_q = rest[12:20]
    s = Names(**dict(zip(names, rest[20 : 20 + len(names)])))
    send_sem, recv_sem, load_sem, out_sem = rest[20 + len(names) :]

    R, D = vis_ref.shape
    Q = query_ref.shape[0]
    H = s.w_win_out.shape[0]
    F = s.w_up.shape[1]
    heads = H // HEAD_DIM
    pairs = heads // 2
    nz = nb // 2
    own = Q // nb
    cut = D // (2 * nb)
    half = D // 2

    p, b, h = lax.axis_index("page"), lax.axis_index("blk"), lax.axis_index("head")
    z, x = b // 2, b % 2
    core = (p, b, 1 - h)
    page = (1 - p, b, h)
    side = (p, z * 2 + (1 - x), h)
    peers = [(p, lax.rem(b + step, nb), h) for step in range(1, nb)]
    line = [(p, lax.rem(z + step, nz) * 2 + x, h) for step in range(1, nz)]

    loads = {}

    def load(name):
        target = getattr(s, FEED_REFS.get(name, name))
        loads[name] = pltpu.make_async_copy(hbm[name], target, load_sem.at[len(loads)])
        loads[name].start()

    for name in LOAD_ORDER:
        load(name)
    barrier = pltpu.get_barrier_semaphore()
    for device in [core, page] + peers:
        pl.semaphore_signal(barrier, inc=1, device_id=device, device_id_type=MESH)

    count = [0]

    def push(src, dst, device):
        at = count[0]
        count[0] += 1
        copy = pltpu.make_async_remote_copy(
            src_ref=src, dst_ref=dst, send_sem=send_sem.at[at], recv_sem=recv_sem.at[at], device_id=device, device_id_type=MESH
        )
        copy.start()
        return copy

    started = []

    def send(src, dst, device):
        copy = push(src, dst, device)
        started.append(copy)
        return copy

    def sent(copy):
        started[:] = [other for other in started if other is not copy]
        copy.wait_send()

    written = []

    def write(src, dst):
        copy = pltpu.make_async_copy(src, dst, out_sem.at[len(written)])
        copy.start()
        written.append(copy)

    lane = iota((1, 128), 1)
    first = lane < HEAD_DIM
    keep = [jnp.where(first, 1.0, 0.0).astype(BF), jnp.where(first, 0.0, 1.0).astype(BF)]
    factor = HEAD_DIM ** (-0.5)
    scaled = [jnp.where(first, factor, 0.0).astype(BF), jnp.where(first, 0.0, factor).astype(BF)]

    def columns(j, width=128):
        if isinstance(j, int):
            return pl.ds(j * width, width)
        return pl.ds(pl.multiple_of(j * width, width), width)

    def pair_loop(body):
        for j in range(pairs):
            body(j)


    def norm(count, step, stream, gain_row, low, hat, inv, keep_ref=None):
        gain = gains_ref[gain_row : gain_row + 1, :]

        def body(ds):
            rows = stream(ds)
            if keep_ref is not None:
                keep_ref[ds, :] = rows
            middle = jnp.mean(rows, axis=-1, keepdims=True)
            centred = rows - middle
            inverse = lax.rsqrt(jnp.mean(centred * centred, axis=-1, keepdims=True) + EPS)
            normal = centred * inverse
            if hat is not None:
                hat[ds, :] = normal
            inv[ds, :] = jnp.where(first, inverse, middle)
            low[ds, :] = (normal * gain).astype(BF)

        row_loop(count, step, body)

    def norm_grad(count, step, before, parts, gain_row, hat, inv, out, low=None):
        gain = gains_ref[gain_row : gain_row + 1, :]

        def body(ds):
            back = parts[0][ds, :] + parts[1][ds, :]
            normal = hat(ds) if callable(hat) else hat[ds, :]
            grown = back * gain
            even = jnp.mean(grown, axis=-1, keepdims=True)
            along = jnp.mean(grown * normal, axis=-1, keepdims=True)
            total = before(ds) + inv[ds, 0:1] * (grown - even - normal * along)
            out[ds, :] = total
            if low is not None:
                low[ds, :] = total.astype(BF)
            return back * normal

        s.gain[gain_row : gain_row + 1, :] = row_sum(count, step, D, body)

    def attend(q, k, v, extra, probs, out):
        def pair(j):
            at = columns(j)
            qp, kp, vp = q[:, at], k[:, at], v[:, at]
            halves = []
            for t in range(2):
                scores = extra(mm_nt(qp * scaled[t], kp), 2 * j + t)
                raised = jnp.exp(scores - jnp.max(scores, axis=-1, keepdims=True))
                prob = raised * (1.0 / jnp.sum(raised, axis=-1, keepdims=True))
                probs[2 * j + t] = prob
                halves.append(mm(prob.astype(BF), vp))
            out[:, at] = jnp.where(first, halves[0], halves[1]).astype(BF)

        pair_loop(pair)

    def attend_back(q, k, v, da, prob_of, put, rowdot=None, hook=None):
        def pair(j):
            at = columns(j)
            qp, kp, vp, dap = q[:, at], k[:, at], v[:, at], da[:, at]
            dq = dk = dv = None
            for t in range(2):
                prob = prob_of(2 * j + t)
                own_da = dap * keep[t]
                dprob = mm_nt(own_da, vp)
                if rowdot is None:
                    delta = jnp.sum(prob * dprob, axis=-1, keepdims=True)
                else:
                    delta = rowdot(dap, j, t)
                ds = prob * (dprob - delta)
                if hook is not None:
                    hook(2 * j + t, ds)
                low = ds.astype(BF)
                parts = (mm(low, kp * scaled[t]), mm_tn(low, qp * scaled[t]), mm_tn(prob.astype(BF), own_da))
                dq, dk, dv = parts if dq is None else (dq + parts[0], dk + parts[1], dv + parts[2])
            put(at, dq, dk, dv)

        pair_loop(pair)

    def feed(low, cot, up, down, dy):
        width = 256

        def body(c):
            at = columns(c, width)
            hidden = mm(low[...], up[:, at])
            grad_act = mm_nt(cot[...], down[at, :])
            spread = 0.5 + 0.5 * lax.erf(hidden * (0.5**0.5))
            bell = jnp.exp(-0.5 * hidden * hidden) * 0.3989422804014327
            dy[:, columns(c + F // width, width)] = (hidden * spread).astype(BF)
            dy[:, at] = (grad_act * (spread + hidden * bell)).astype(BF)

        loop(F // width, body)

    def left(pieces, mine):
        for at, piece in enumerate(pieces):
            s.x_out[at] = mm_nt(s.sel[1], piece[...]).astype(BF)
            mine[at] = mm_nt(s.sel[0], piece[...]).astype(BF)

    def weight_grads(mine, other, dy, dy_in, split, panels):
        for n, panel in enumerate(panels):
            width = 384
            for c in range(D // width):
                low = n * D + c * width
                at = 0 if low < split else 1
                cols = pl.ds(low, width)
                value = mm(mine[at], dy[:, cols]) + mm(other[at], dy_in[:, cols])
                panel[:, pl.ds(c * width, width)] = value.astype(BF)

    def side_push(panels, incoming):
        theirs = pl.ds(pl.multiple_of((1 - x) * (half // 2), half // 2), half // 2)
        return [send(panel.at[theirs], incoming.at[n], side) for n, panel in enumerate(panels)]

    def block_rows(at):
        return pl.ds(pl.multiple_of(at * cut, cut), cut)

    def line_push(panels, incoming, out, arrive):
        copies = []
        for step in range(1, nz):
            to = lax.rem(z + step, nz)
            rows = pl.ds((step - 1) * cut, cut)
            for n, panel in enumerate(panels):
                total = panel[block_rows(x * nz + to), :].astype(F32) + incoming[n, block_rows(to), :].astype(F32)
                out[rows, pl.ds(n * D, D)] = total.astype(BF)
            copies.append(send(out.at[rows], arrive.at[step - 1], line[step - 1]))
        return copies

    def line_sum(panels, incoming, arrive, offset):
        for n, panel in enumerate(panels):
            total = panel[block_rows(x * nz + z), :].astype(F32) + incoming[n, block_rows(z), :].astype(F32)
            for step in range(1, nz):
                total = total + arrive[step - 1, :, pl.ds(n * D, D)].astype(F32)
            s.slab_v[:, pl.ds(offset + n * D, D)] = total
        section = pl.ds(offset, D * len(panels))
        write(s.slab_v.at[:, section], out_v.at[:, section])

    def query_grads(piece, dy, dy_at, size, offset, out, out_at):
        turned = mm_nt(s.sel_q[...], piece[...]).astype(BF)
        width = 384
        for c in range(size // width):
            value = mm(turned, dy[:, pl.ds(dy_at + c * width, width)])
            s.slab_q[:, pl.ds(offset + c * width, width)] = value[:cut]
            out[:, pl.ds(out_at + c * width, width)] = value[cut:].astype(BF)

    def add_query(arrive, offset):
        width = 768
        size = arrive.shape[1]
        for c in range(size // width):
            s.slab_q[:, pl.ds(offset + c * width, width)] += arrive[:, pl.ds(c * width, width)].astype(F32)
        section = pl.ds(offset, size)
        write(s.slab_q.at[:, section], out_q.at[:, section])

    def split_dot(product, values, ones):
        total = None
        for _ in range(3):
            part = values.astype(BF)
            values = values - part.astype(F32)
            share = product(part, ones)
            total = share if total is None else total + share
        return total

    def store(ref, ds, value):
        ref[ds, :] = value.astype(ref.dtype)

    RV, RQ = 48, 32

    for at, start in enumerate((p * half, (1 - p) * half)):
        for place in range(nb):
            block = (place % nz) * 2 + place // nz
            rows = pl.ds(place * cut, cut)
            s.sel[at, rows, :] = (iota((cut, D), 1) == iota((cut, D), 0) + (start + block * cut)).astype(BF)
    rows = iota((2 * cut, D), 0)
    start = jnp.where(rows < cut, (p * nb + b) * cut, ((1 - p) * nb + b) * cut - cut)
    s.sel_q[...] = (iota((2 * cut, D), 1) == rows + start).astype(BF)

    index = iota((STRIP_LANES, 1), 0)
    outer = ((index.astype(F32) + 0.5) * (1.0 / WIN)).astype(jnp.int32)
    target = (2 * WIN - 2 - outer) * DIFFS + (WIN - 1) - (index - outer * WIN)
    target = jnp.where(index < DIFFS * WIN, target, -1)
    s.hot[...] = (iota((STRIP_LANES, TABLE_LANES), 1) == target).astype(BF)
    s.rolled[...] = jnp.zeros(s.rolled.shape, F32)
    for px in range(WIN):
        turned = table_ref[...] if px == 0 else pltpu.roll(table_ref[...], TABLE_LANES - px, 1)
        for head in range(heads):
            s.rolled[head, px : px + 1, :] = turned[head : head + 1, :]
    for head in range(heads):
        s.strip[head] = split_dot(mm_nt, s.rolled[head], s.hot[...])
    for py in range(WIN):
        at = (WIN - 1 - py) * WIN
        s.bias[:, py * WIN : (py + 1) * WIN, :] = s.strip[:, 0:WIN, at : at + AREA]

    position = iota((1, Q), 1)
    alive = position < length_ref[0]
    norm(Q, RQ, lambda ds: query_ref[ds, :].astype(F32), 1, s.cau_low, None, s.cau_inv)
    loads["w_cau"].wait()
    for i in range(3):
        s.cau_qkv[i] = mm(s.cau_low[...], s.w_cau[i]).astype(BF)
    causal_live = (iota((Q, Q), 1) <= iota((Q, Q), 0)) & alive
    attend(
        s.cau_qkv.at[0], s.cau_qkv.at[1], s.cau_qkv.at[2],
        lambda scores, head: jnp.where(causal_live, scores, -jnp.inf), s.cau_p, s.cau_att,
    )
    loads["w_cau_out"].wait()
    s.a_q[...] = mm(s.cau_att[...], s.w_cau_out[...])
    pl.semaphore_wait(barrier, nb + 1)
    a_q = send(s.a_q, s.a_q_in, core)

    norm(R, RV, lambda ds: vis_ref[ds, :].astype(F32), 0, s.win_low, None, s.win_inv)
    loads["w_win"].wait()
    for i in range(3):
        s.win_qkv[i] = mm(s.win_low[...], s.w_win[i]).astype(BF)
    win_att = s.dyw.at[:, pl.ds(3 * H, H)]
    attend(
        s.win_qkv.at[0], s.win_qkv.at[1], s.win_qkv.at[2],
        lambda scores, head: scores + s.bias[head], s.win_p, win_att,
    )
    loads["w_win_out"].wait()
    s.a_v[...] = mm(win_att[...], s.w_win_out[...])
    a_v = send(s.a_v, s.a_v_in, core)

    a_q.wait_recv()
    norm(
        Q, RQ, lambda ds: query_ref[ds, :].astype(F32) + (s.a_q[ds, :] + s.a_q_in[ds, :]),
        2, s.cq_low, s.cq_hat, s.cq_inv, s.que1,
    )
    loads["w_read"].wait()
    loads["w_write"].wait()
    s.read_q[...] = mm(s.cq_low[...], s.w_read[0]).astype(BF)
    s.write_kv[0] = mm(s.cq_low[...], s.w_write[1]).astype(BF)
    s.write_kv[1] = mm(s.cq_low[...], s.w_write[2]).astype(BF)
    a_v.wait_recv()
    norm(
        R, RV, lambda ds: vis_ref[ds, :].astype(F32) + (s.a_v[ds, :] + s.a_v_in[ds, :]),
        3, s.cv_low, s.cv_hat, s.cv_inv, s.vis1,
    )
    s.read_kv[0] = mm(s.cv_low[...], s.w_read[1]).astype(BF)
    s.read_kv[1] = mm(s.cv_low[...], s.w_read[2]).astype(BF)
    s.write_q[...] = mm(s.cv_low[...], s.w_write[0]).astype(BF)

    stats = jnp.broadcast_to(jnp.where(lane < HEAD_DIM, 0.0, 1.0), (Q, 128))
    for j in range(pairs):
        at = columns(j)
        qp, kp, vp = s.read_q[:, at], s.read_kv[0, :, at], s.read_kv[1, :, at]
        halves = []
        for t in range(2):
            head = 2 * j + t
            scores = mm_nt(qp * scaled[t], kp)
            peak = jnp.max(scores, axis=-1, keepdims=True)
            raised = jnp.exp(scores - peak)
            s.read_p[head] = raised
            stats = jnp.where(lane == head, peak, stats)
            stats = jnp.where(lane == HEAD_DIM + head, jnp.sum(raised, axis=-1, keepdims=True), stats)
            halves.append(mm(raised.astype(BF), vp))
        s.part[:, at] = jnp.where(first, halves[0], halves[1])
    s.part[:, H:] = stats

    def own_rows(device):
        return pl.ds(pl.multiple_of(device * own, own), own)

    mine = own_rows(b)
    part_copies = [send(s.part.at[own_rows(peer[1])], s.part_in.at[step], peer) for step, peer in enumerate(peers)]

    att_w = s.dyc.at[:, pl.ds(3 * H, H)]
    attend(
        s.write_q, s.write_kv.at[0], s.write_kv.at[1],
        lambda scores, head: jnp.where(alive, scores, -jnp.inf), s.write_p, att_w,
    )
    loads["w_write_out"].wait()
    s.b_v[...] = mm(att_w[...], s.w_write_out[...])
    b_v = send(s.b_v, s.b_v_in, core)

    for copy in part_copies:
        copy.wait_recv()
    sources = [s.part.at[mine]] + [s.part_in.at[step] for step in range(nb - 1)]
    peak = None
    for source in sources:
        peak = source[:, H:] if peak is None else jnp.maximum(peak, source[:, H:])
    mass = jnp.zeros((own, 128), F32)
    grown = []
    for source in sources:
        share = jnp.exp(source[:, H:] - peak)
        grown.append(share)
        mass = mass + share * pltpu.roll(source[:, H:], HEAD_DIM, 1)
    known = lane < heads
    mass = jnp.where(known, mass, 1.0)
    over = 1.0 / mass
    for j in range(pairs):
        at = columns(j)
        total = jnp.zeros((own, 128), F32)
        for source, share in zip(sources, grown):
            weight = share * over
            total = total + source[:, at] * jnp.where(first, weight[:, 2 * j : 2 * j + 1], weight[:, 2 * j + 1 : 2 * j + 2])
        s.mix[mine, at] = total
    s.mix[mine, H:] = jnp.where(known, peak + jnp.log(mass), 0.0)
    mix_copies = [send(s.mix.at[mine], s.mix.at[mine], peer) for peer in peers]

    b_v.wait_recv()
    norm(
        R, RV, lambda ds: s.vis1[ds, :] + (s.b_v[ds, :] + s.b_v_in[ds, :]), 4, s.fv_low, s.fv_hat, s.fv_inv, s.vis2
    )
    loads["w_vdown"].wait()
    loads["w_vup"].wait()
    feed(s.fv_low, cotv_ref, s.w_up, s.w_down, s.dyf)
    sent(a_v)
    s.a_v[...] = mm_nt(s.dyf[:, :F], s.w_up[...])
    d_v = send(s.a_v, s.a_v_in, core)
    load("w_qup")
    sent(b_v)
    s.b_v[...] = mm(s.dyf[:, F:], s.w_down[...])
    load("w_qdown")

    for copy in mix_copies:
        copy.wait_recv()
    s.read_att[...] = s.mix[:, :H].astype(BF)
    loads["w_read_out"].wait()
    s.b_q[...] = mm(s.read_att[...], s.w_read_out[...])
    b_q = send(s.b_q, s.b_q_in, core)

    left((s.fv_low, cotv_ref), s.xf)
    xf = send(s.x_out, s.xf_in, page)
    dyf = send(s.dyf, s.dyf_in, page)

    b_q.wait_recv()
    norm(
        Q, RQ, lambda ds: s.que1[ds, :] + (s.b_q[ds, :] + s.b_q_in[ds, :]), 5, s.fq_low, s.fq_hat, s.fq_inv, s.que2
    )
    loads["w_qdown"].wait()
    loads["w_qup"].wait()
    feed(s.fq_low, cotq_ref, s.w_up, s.w_down, s.dyq)
    sent(a_q)
    s.a_q[...] = mm_nt(s.dyq[:, :F], s.w_up[...])
    d_q = send(s.a_q, s.a_q_in, core)

    d_v.wait_recv()
    norm_grad(
        R, RV, lambda ds: cotv_ref[ds, :].astype(F32), (s.a_v, s.a_v_in), 4, s.fv_hat, s.fv_inv, s.vis1, s.gvis2_low
    )
    c_v = send(s.b_v, s.b_v_in, core)
    s.da_v[...] = mm_nt(s.gvis2_low[...], s.w_write_out[...]).astype(BF)

    def put_write(at, dq, dk, dv):
        s.dyc[:, at] = dq.astype(BF)
        s.qg[:, pl.ds(at.start + H, 128)] = dk
        s.qg[:, pl.ds(at.start + 2 * H, 128)] = dv

    attend_back(s.write_q, s.write_kv.at[0], s.write_kv.at[1], s.da_v, lambda head: s.write_p[head], put_write)

    sent(b_q)
    s.b_q[...] = mm(s.dyq[:, F:], s.w_down[...])
    d_q.wait_recv()
    norm_grad(
        Q, RQ, lambda ds: cotq_ref[ds, :].astype(F32), (s.a_q, s.a_q_in), 5, s.fq_hat, s.fq_inv, s.que1, s.gque2_low
    )
    c_q = send(s.b_q, s.b_q_in, core)
    s.da_q[...] = mm_nt(s.gque2_low[...], s.w_read_out[...]).astype(BF)

    def read_prob(head):
        moved = jnp.exp(s.part[:, H + head : H + head + 1] - s.mix[:, H + head : H + head + 1])
        return s.read_p[head] * moved

    def read_rowdot(dap, j, t):
        return jnp.sum((dap * keep[t]).astype(F32) * s.mix[:, columns(j)], axis=-1, keepdims=True)

    def put_read(at, dq, dk, dv):
        s.qg[:, at] = dq
        s.dyc[:, pl.ds(at.start + H, 128)] = dk.astype(BF)
        s.dyc[:, pl.ds(at.start + 2 * H, 128)] = dv.astype(BF)

    attend_back(s.read_q, s.read_kv.at[0], s.read_kv.at[1], s.da_q, read_prob, put_read, read_rowdot)
    qg_copies = [send(s.qg.at[own_rows(peer[1])], s.qg_in.at[step], peer) for step, peer in enumerate(peers)]

    c_v.wait_recv()
    row_loop(R, RV, lambda ds: store(s.fv_low, ds, s.vis2[ds, :] + (s.b_v[ds, :] + s.b_v_in[ds, :])))
    write(s.fv_low, vis_out)
    sent(d_v)
    s.a_v[...] = (
        mm_nt(s.dyc[:, :H], s.w_write[0]) + mm_nt(s.dyc[:, H : 2 * H], s.w_read[1]) + mm_nt(s.dyc[:, 2 * H : 3 * H], s.w_read[2])
    )
    e_v = send(s.a_v, s.a_v_in, core)

    f_panels = [s.w_down.at[pl.ds(n * half, half)] for n in range(4)]
    c_panels = [s.w_up.at[pl.ds(0, half), pl.ds(n * D, D)] for n in range(2)]
    w_panels = [s.w_up.at[pl.ds(half, half), pl.ds(n * D, D)] for n in range(2)]
    xf.wait_recv()
    dyf.wait_recv()
    weight_grads(s.xf, s.xf_in, s.dyf, s.dyf_in, F, f_panels)
    gf = side_push(f_panels, s.gf_in)
    sent(xf)
    left((s.cv_low, s.gvis2_low), s.xc)
    xc = send(s.x_out, s.xc_in, page)
    dyc = send(s.dyc, s.dyc_in, page)
    query_grads(s.fq_low, s.dyq, 0, F, 0, s.tf, 0)
    query_grads(cotq_ref, s.dyq, F, F, F, s.tf, F)
    tf = send(s.tf, s.tf_in, page)

    e_v.wait_recv()
    norm_grad(R, RV, lambda ds: s.vis1[ds, :], (s.a_v, s.a_v_in), 3, s.cv_hat, s.cv_inv, s.vis1, s.gvis1_low)
    s.da_v[...] = mm_nt(s.gvis1_low[...], s.w_win_out[...]).astype(BF)

    def put_window(at, dq, dk, dv):
        s.dyw[:, at] = dq.astype(BF)
        s.dyw[:, pl.ds(at.start + H, 128)] = dk.astype(BF)
        s.dyw[:, pl.ds(at.start + 2 * H, 128)] = dv.astype(BF)

    def table_hook(head, ds):
        s.bias[head] = ds

    attend_back(
        s.win_qkv.at[0], s.win_qkv.at[1], s.win_qkv.at[2], s.da_v, lambda head: s.win_p[head], put_window, hook=table_hook
    )
    sent(c_v)
    s.b_v[...] = mm_nt(s.dyw[:, :H], s.w_win[0]) + mm_nt(s.dyw[:, H : 2 * H], s.w_win[1]) + mm_nt(s.dyw[:, 2 * H : 3 * H], s.w_win[2])
    f_v = send(s.b_v, s.b_v_in, core)
    sent(xc)
    left((s.win_low, s.gvis1_low), s.xw)
    xw = send(s.x_out, s.xw_in, page)
    dyw = send(s.dyw, s.dyw_in, page)

    for copy in qg_copies:
        copy.wait_recv()
    for c in range(3):
        at = pl.ds(c * H, H)
        total = s.qg[mine, at]
        for step in range(nb - 1):
            total = total + s.qg_in[step, :, at]
        s.qg_low[mine, at] = total.astype(BF)
    low_copies = [send(s.qg_low.at[mine], s.qg_low.at[mine], peer) for peer in peers]

    s.strip[...] = jnp.zeros(s.strip.shape, F32)
    for py in range(WIN):
        at = (WIN - 1 - py) * WIN
        s.strip[:, 0:WIN, at : at + AREA] += s.bias[:, py * WIN : (py + 1) * WIN, :]
    for head in range(heads):
        s.rolled[head] = split_dot(mm, s.strip[head], s.hot[...])
    s.tab[...] = jnp.zeros(s.tab.shape, F32)
    for head in range(heads):
        total = s.rolled[head, 0:1, :]
        for px in range(1, WIN):
            total = total + pltpu.roll(s.rolled[head, px : px + 1, :], px, 1)
        s.tab[head : head + 1, :] = total
    tab = send(s.tab, s.tab_in, page)

    for copy in gf:
        copy.wait_recv()
    zf = line_push(f_panels, s.gf_in, s.dyq, s.zf_in)

    c_q.wait_recv()
    row_loop(Q, RQ, lambda ds: store(s.fq_low, ds, s.que2[ds, :] + (s.b_q[ds, :] + s.b_q_in[ds, :])))
    write(s.fq_low, query_out)
    for copy in low_copies:
        copy.wait_recv()
    sent(d_q)
    s.a_q[...] = (
        mm_nt(s.qg_low[:, :H], s.w_read[0]) + mm_nt(s.qg_low[:, H : 2 * H], s.w_write[1]) + mm_nt(s.qg_low[:, 2 * H :], s.w_write[2])
    )
    e_q = send(s.a_q, s.a_q_in, core)
    xc.wait_recv()
    dyc.wait_recv()
    weight_grads(s.xc, s.xc_in, s.dyc, s.dyc_in, 3 * H, c_panels)
    gc = side_push(c_panels, s.gc_in)
    e_q.wait_recv()
    norm_grad(Q, RQ, lambda ds: s.que1[ds, :], (s.a_q, s.a_q_in), 2, s.cq_hat, s.cq_inv, s.que1, s.gque1_low)
    s.da_q[...] = mm_nt(s.gque1_low[...], s.w_cau_out[...]).astype(BF)

    def put_causal(at, dq, dk, dv):
        s.cau_g[:, at] = dq.astype(BF)
        s.cau_g[:, pl.ds(at.start + H, 128)] = dk.astype(BF)
        s.cau_g[:, pl.ds(at.start + 2 * H, 128)] = dv.astype(BF)

    attend_back(s.cau_qkv.at[0], s.cau_qkv.at[1], s.cau_qkv.at[2], s.da_q, lambda head: s.cau_p[head], put_causal)
    sent(c_q)
    s.b_q[...] = (
        mm_nt(s.cau_g[:, :H], s.w_cau[0]) + mm_nt(s.cau_g[:, H : 2 * H], s.w_cau[1]) + mm_nt(s.cau_g[:, 2 * H :], s.w_cau[2])
    )
    f_q = send(s.b_q, s.b_q_in, core)

    xw.wait_recv()
    dyw.wait_recv()
    weight_grads(s.xw, s.xw_in, s.dyw, s.dyw_in, 3 * H, w_panels)
    gw = side_push(w_panels, s.gw_in)

    base = 2 * F
    query_grads(s.cq_low, s.qg_low, 0, 3 * H, base, s.tc, 0)
    query_grads(s.gque2_low, s.read_att, 0, H, base + 3 * H, s.tc, 3 * H)
    tc = send(s.tc, s.tc_in, page)
    base = 2 * F + 4 * H
    query_grads(s.cau_low, s.cau_g, 0, 3 * H, base, s.tw, 0)
    query_grads(s.gque1_low, s.cau_att, 0, H, base + 3 * H, s.tw, 3 * H)
    tw = send(s.tw, s.tw_in, page)

    def hat_of(stream, inv):
        return lambda ds: (stream[ds, :].astype(F32) - inv[ds, HEAD_DIM : HEAD_DIM + 1]) * inv[ds, 0:1]

    f_v.wait_recv()
    norm_grad(R, RV, lambda ds: s.vis1[ds, :], (s.b_v, s.b_v_in), 0, hat_of(vis_ref, s.win_inv), s.win_inv, s.vis1)
    write(s.vis1, grad_vis)
    f_q.wait_recv()
    norm_grad(Q, RQ, lambda ds: s.que1[ds, :], (s.b_q, s.b_q_in), 1, hat_of(query_ref, s.cau_inv), s.cau_inv, s.que1)
    write(s.que1, grad_query)
    s.gain[6:8, :] = jnp.zeros((2, D), F32)
    gain = send(s.gain, s.gain_in, page)

    for copy in gc:
        copy.wait_recv()
    sent(dyf)
    zc = line_push(c_panels, s.gc_in, s.dyf.at[:, pl.ds(0, 4 * H)], s.zc_in)

    tab.wait_recv()
    s.tab_page[...] = s.tab[...] + s.tab_in[...]
    tab_copies = [send(s.tab_page, s.tab_blk.at[step], peer) for step, peer in enumerate(peers)]
    gain.wait_recv()
    s.gain_page[...] = s.gain[...] + s.gain_in[...]
    gain_copies = [send(s.gain_page, s.gain_blk.at[step], peer) for step, peer in enumerate(peers)]

    for copy in gw:
        copy.wait_recv()
    zw = line_push(w_panels, s.gw_in, s.dyf.at[:, pl.ds(4 * H, 4 * H)], s.zw_in)

    for copy in zf:
        copy.wait_recv()
    line_sum(f_panels, s.gf_in, s.zf_in, 0)
    tf.wait_recv()
    add_query(s.tf_in, 0)
    tc.wait_recv()
    add_query(s.tc_in, 2 * F)
    tw.wait_recv()
    add_query(s.tw_in, 2 * F + 4 * H)
    for copy in zc:
        copy.wait_recv()
    line_sum(c_panels, s.gc_in, s.zc_in, 2 * F)

    for copy in tab_copies:
        copy.wait_recv()
    total = s.tab_page[...]
    for step in range(nb - 1):
        total = total + s.tab_blk[step]
    table_out[...] = total
    for copy in gain_copies:
        copy.wait_recv()
    total = s.gain_page[...]
    for step in range(nb - 1):
        total = total + s.gain_blk[step]
    row = iota((8, 1), 0)
    from_query = (row == 1) | (row == 2) | (row == 5)
    total = jnp.where(from_query, s.gain_page[...], total)
    pick = (iota((D, 128), 0) == iota((D, 128), 1) + (p * nb + b) * cut).astype(BF)
    gain_out[...] = split_dot(mm, total, pick)

    for copy in zw:
        copy.wait_recv()
    line_sum(w_panels, s.gw_in, s.zw_in, 2 * F + 4 * H)
    for copy in list(started):
        sent(copy)
    for copy in written:
        copy.wait()


def finish_kernel(H, F, cut, *refs):
    vis_in, query_in, gvis_in, gque_in, gain_in, slab_v, slab_q = refs[:7]
    (
        vis_out, query_out, gvis_out, gque_out, gain_out, win_qkv, win_out, cau_qkv, cau_out, read_qkv, read_out, write_qkv,
        write_out, vis_up, vis_down, query_up, query_down,
    ) = refs[7:]
    vis_out[...] = vis_in[...]
    query_out[...] = query_in[...]
    gvis_out[...] = gvis_in[...]
    gque_out[...] = gque_in[...]
    gain_out[...] = gain_in[:6, :cut]

    def turned(ref, at, size):
        return jnp.transpose(ref[:, at : at + size], (1, 0))

    vis_up[...] = slab_v[:, :F]
    vis_down[...] = turned(slab_v, F, F)
    query_up[...] = slab_q[:, :F]
    query_down[...] = turned(slab_q, F, F)
    cross, last = 2 * F, 2 * F + 4 * H
    for i in range(3):
        win_qkv[i] = slab_v[:, last + i * H : last + (i + 1) * H]
        cau_qkv[i] = slab_q[:, last + i * H : last + (i + 1) * H]
    win_out[...] = turned(slab_v, last + 3 * H, H)
    cau_out[...] = turned(slab_q, last + 3 * H, H)
    write_qkv[0] = slab_v[:, cross : cross + H]
    read_qkv[1] = slab_v[:, cross + H : cross + 2 * H]
    read_qkv[2] = slab_v[:, cross + 2 * H : cross + 3 * H]
    write_out[...] = turned(slab_v, cross + 3 * H, H)
    read_qkv[0] = slab_q[:, cross : cross + H]
    write_qkv[1] = slab_q[:, cross + H : cross + 2 * H]
    write_qkv[2] = slab_q[:, cross + 2 * H : cross + 3 * H]
    read_out[...] = turned(slab_q, cross + 3 * H, H)


ANY_SPEC = pl.BlockSpec(memory_space=pl.ANY)
VMEM_SPEC = pl.BlockSpec(memory_space=pltpu.VMEM)


def fused_shards(
    vis_tokens, query_tokens, answer_lengths, norm_gains, bias_table, window_qkv, window_out, causal_qkv, causal_out,
    read_qkv, read_out, write_qkv, write_out, vis_up, vis_down, query_up, query_down, cot_vis, cot_query,
):
    nb = lax.axis_size("blk")
    R, D = vis_tokens.shape[1:]
    Q = query_tokens.shape[1]
    H, F = window_out.shape[0], vis_up.shape[1]
    own, cut = Q // nb, D // (2 * nb)
    heads = H // HEAD_DIM
    table = jnp.pad(bias_table.reshape(heads, DIFFS * DIFFS), ((0, 8 - heads), (0, TABLE_LANES - DIFFS * DIFFS)))
    scratch = scratch_shapes(R, Q, D, H, F, nb, own, cut)
    names = tuple(scratch)
    sems = 160
    slab = jax.ShapeDtypeStruct((cut, 2 * F + 8 * H), F32)
    shape = jax.ShapeDtypeStruct
    pieces = pl.pallas_call(
        partial(block_kernel, names, nb),
        out_shape=(
            shape((R, D), BF), shape((Q, D), BF), shape((R, D), F32), shape((Q, D), F32), shape((8, 128), F32),
            shape((8, TABLE_LANES), F32), slab, slab,
        ),
        in_specs=[VMEM_SPEC, VMEM_SPEC, pl.BlockSpec(memory_space=pltpu.SMEM), VMEM_SPEC, VMEM_SPEC, VMEM_SPEC, VMEM_SPEC]
        + [ANY_SPEC] * 12,
        out_specs=[ANY_SPEC] * 4 + [VMEM_SPEC] * 2 + [ANY_SPEC] * 2,
        scratch_shapes=[pltpu.VMEM(dims, dtype) for dims, dtype in scratch.values()]
        + [pltpu.SemaphoreType.DMA((sems,)), pltpu.SemaphoreType.DMA((sems,)), pltpu.SemaphoreType.DMA((12,)), pltpu.SemaphoreType.DMA((16,))],
        compiler_params=pltpu.CompilerParams(collective_id=0, has_side_effects=True, vmem_limit_bytes=VMEM_LIMIT),
        name="block",
    )(
        vis_tokens[0], query_tokens[0], answer_lengths, norm_gains, table, cot_vis[0], cot_query[0], window_qkv, window_out,
        causal_qkv, causal_out, read_qkv, read_out, write_qkv, write_out, vis_up, vis_down, query_up, query_down,
    )
    vis_part, query_part, gvis, gque, gain, tab, slab_v, slab_q = pieces
    outs = pl.pallas_call(
        partial(finish_kernel, H, F, cut),
        out_shape=(
            shape((R, D), BF), shape((Q, D), BF), shape((R, D), F32), shape((Q, D), F32), shape((6, cut), F32),
            shape((3, cut, H), F32), shape((H, cut), F32), shape((3, cut, H), F32), shape((H, cut), F32),
            shape((3, cut, H), F32), shape((H, cut), F32), shape((3, cut, H), F32), shape((H, cut), F32),
            shape((cut, F), F32), shape((F, cut), F32), shape((cut, F), F32), shape((F, cut), F32),
        ),
        in_specs=[VMEM_SPEC] * 7,
        out_specs=[VMEM_SPEC] * 17,
        compiler_params=pltpu.CompilerParams(vmem_limit_bytes=VMEM_LIMIT),
        name="finish",
    )(vis_part, query_part, gvis, gque, gain, slab_v, slab_q)
    table_grad = tab[:heads, : DIFFS * DIFFS].reshape(heads, DIFFS, DIFFS)
    return (outs[0][None], outs[1][None], outs[2][None], outs[3][None], outs[4], table_grad) + tuple(outs[5:])


VMEM_LIMIT = 60 * 2**20


def combined_all(value, axis, join):
    pieces = jax.tree.map(lambda part: lax.all_gather(part, axis), value)
    head = jax.tree.map(lambda part: part[0], pieces)
    tail = jax.tree.map(lambda part: part[1:], pieces)
    subtotal, _ = lax.scan(lambda subtotal, section: (join(subtotal, section), None), head, tail)
    return subtotal


def matmul(matrix, other):
    return jnp.dot(matrix, other, preferred_element_type=jnp.float32)


def times_back(matrix, other):
    return lax.dot_general(
        matrix, other, (((1,), (1,)), ((), ())), preferred_element_type=jnp.float32
    )


def inner_rows(matrix, other):
    return lax.dot_general(
        matrix, other, (((0,), (0,)), ((), ())), preferred_element_type=jnp.float32
    )


def layer_norm(stream, gain):
    centred = stream - jnp.mean(stream, axis=-1, keepdims=True)
    inverse = lax.rsqrt(jnp.mean(centred * centred, axis=-1, keepdims=True) + EPS)
    normal = centred * inverse
    return (normal * gain, normal, inverse)


def norm_back(grad_out, normal, inverse, gain):
    scaled = grad_out * gain
    return inverse * (
        scaled
        - jnp.mean(scaled, axis=-1, keepdims=True)
        - normal * jnp.mean(scaled * normal, axis=-1, keepdims=True)
    )


def scores_of(queries, keyset, factor):
    return (
        jnp.einsum("bqhe,bkhe->bhqk", queries, keyset, preferred_element_type=jnp.float32) * factor
    )


def attend(queries, keyset, values, additive, factor):
    scores = scores_of(queries, keyset, factor) + additive
    peak_val = jnp.max(scores, axis=-1, keepdims=True)
    log_total = peak_val + jnp.log(jnp.sum(jnp.exp(scores - peak_val), axis=-1, keepdims=True))
    soft_probs = jnp.exp(scores - log_total).astype(jnp.bfloat16)
    mix_out = jnp.einsum("bhqk,bkhe->bqhe", soft_probs, values, preferred_element_type=jnp.float32)
    return (mix_out, log_total)


def attend_back(grad_low, queries, keyset, values, additive, log_total, factor, reduce_rows):
    scores = scores_of(queries, keyset, factor) + additive
    soft_probs = jnp.exp(scores - log_total)
    grad_probs = jnp.einsum("bqhe,bkhe->bhqk", grad_low, values, preferred_element_type=jnp.float32)
    grad_values = jnp.einsum(
        "bhqk,bqhe->bkhe",
        soft_probs.astype(jnp.bfloat16),
        grad_low,
        preferred_element_type=jnp.float32,
    )
    rowdot = reduce_rows(jnp.sum(soft_probs * grad_probs, axis=-1, keepdims=True))
    grad_scores = soft_probs * (grad_probs - rowdot)
    rounded = grad_scores.astype(jnp.bfloat16)
    grad_queries = (
        jnp.einsum("bhqk,bkhe->bqhe", rounded, keyset, preferred_element_type=jnp.float32) * factor
    )
    grad_keys = (
        jnp.einsum("bhqk,bqhe->bkhe", rounded, queries, preferred_element_type=jnp.float32) * factor
    )
    return (grad_queries, grad_keys, grad_values, grad_scores)


def join_softmax(earlier, later):
    peak_val = jnp.maximum(earlier[0], later[0])
    return (
        peak_val,
        earlier[1] * jnp.exp(earlier[0] - peak_val) + later[1] * jnp.exp(later[0] - peak_val),
    )


def feed_back(grad_out, normed_low, hidden, act_low, up_weight, down_weight, select):
    grad_low = grad_out.astype(jnp.bfloat16)
    grad_act = times_back(grad_low, down_weight)
    grad_down = inner_rows(select(act_low), select(grad_low))
    (grad_hidden,) = jax.vjp(exact_gelu, hidden)[1](grad_act)
    hidden_low = grad_hidden.astype(jnp.bfloat16)
    grad_up = inner_rows(select(normed_low), select(hidden_low))
    return (times_back(hidden_low, up_weight), grad_up, grad_down)


def shards(
    vis_tokens,
    query_tokens,
    answer_lengths,
    norm_gains,
    bias_table,
    window_qkv,
    window_out,
    causal_qkv,
    causal_out,
    read_qkv,
    read_out,
    write_qkv,
    write_out,
    vis_up,
    vis_down,
    query_up,
    query_down,
    cot_vis,
    cot_query,
):
    factor = HEAD_DIM ** (-0.5)
    vis_in = vis_tokens[0].astype(jnp.float32)
    query_in = query_tokens[0].astype(jnp.float32)
    length = answer_lengths[0]
    vis_rows = vis_in.shape[0]
    query_rows = query_in.shape[0]
    local_heads = window_out.shape[0] // HEAD_DIM
    win_area = WIN * WIN
    windows = vis_rows // win_area
    own_rows = query_rows // lax.axis_size("blk")
    first_row = lax.axis_index("blk") * own_rows

    def split(tensor, count):
        return tensor.reshape(count, -1, local_heads, HEAD_DIM)

    def project(normed_low, weight, count):
        return split(matmul(normed_low, weight).astype(jnp.bfloat16), count)

    def flat_low(tensor, count_rows):
        return tensor.reshape(count_rows, -1).astype(jnp.bfloat16)

    def own(tensor):
        return lax.dynamic_slice_in_dim(tensor, first_row, own_rows, 0)

    def same(tensor):
        return tensor

    def head_total(first_part, second_part):
        return lax.psum((first_part, second_part), "head")

    offsets = jnp.arange(WIN)
    one_hot = (
        (offsets[:, None] - offsets[None, :] + WIN - 1)[:, :, None]
        == jnp.arange(2 * WIN - 1)[None, None, :]
    ).astype(jnp.float32)
    rel_bias = jnp.einsum(
        "pqa,rsb,hab->hprqs", one_hot, one_hot, bias_table, precision=HIGH
    ).reshape(local_heads, win_area, win_area)
    window_extra = rel_bias[None]
    positions = jnp.arange(query_rows)
    causal_extra = jnp.where(
        (positions[None, :] <= positions[:, None]) & (positions[None, :] < length), 0.0, -jnp.inf
    )[None, None]
    write_extra = jnp.where(positions < length, 0.0, -jnp.inf)[None, None, None, :]
    window_norm, window_hat, window_inv = layer_norm(vis_in, norm_gains[0])
    window_low = window_norm.astype(jnp.bfloat16)
    window_query = project(window_low, window_qkv[0], windows)
    window_keys = project(window_low, window_qkv[1], windows)
    window_values = project(window_low, window_qkv[2], windows)
    window_mix, window_lse = attend(window_query, window_keys, window_values, window_extra, factor)
    window_att = flat_low(window_mix, vis_rows)
    causal_norm, causal_hat, causal_inv = layer_norm(query_in, norm_gains[1])
    causal_low = causal_norm.astype(jnp.bfloat16)
    causal_query = project(causal_low, causal_qkv[0], 1)
    causal_keys = project(causal_low, causal_qkv[1], 1)
    causal_values = project(causal_low, causal_qkv[2], 1)
    causal_mix, causal_lse = attend(causal_query, causal_keys, causal_values, causal_extra, factor)
    causal_att = flat_low(causal_mix, query_rows)
    window_sum, causal_sum = head_total(
        matmul(window_att, window_out), matmul(causal_att, causal_out)
    )
    vis_one = vis_in + window_sum
    query_one = query_in + causal_sum
    cross_query_norm, cross_query_hat, cross_query_inv = layer_norm(query_one, norm_gains[2])
    cross_query_low = cross_query_norm.astype(jnp.bfloat16)
    cross_vis_norm, cross_vis_hat, cross_vis_inv = layer_norm(vis_one, norm_gains[3])
    cross_vis_low = cross_vis_norm.astype(jnp.bfloat16)
    read_query = project(cross_query_low, read_qkv[0], 1)
    read_keys = project(cross_vis_low, read_qkv[1], 1)
    read_values = project(cross_vis_low, read_qkv[2], 1)
    write_query = project(cross_vis_low, write_qkv[0], 1)
    write_keys = project(cross_query_low, write_qkv[1], 1)
    write_values = project(cross_query_low, write_qkv[2], 1)
    read_scores = scores_of(read_query, read_keys, factor)
    peak_val = jnp.max(read_scores, axis=-1, keepdims=True)
    mass = jnp.sum(jnp.exp(read_scores - peak_val), axis=-1, keepdims=True)
    peak_val, mass = combined_all((peak_val, mass), "blk", join_softmax)
    read_lse = peak_val + jnp.log(mass)
    read_probs = jnp.exp(read_scores - read_lse).astype(jnp.bfloat16)
    read_part = jnp.einsum(
        "bhqk,bkhe->bqhe", read_probs, read_values, preferred_element_type=jnp.float32
    )
    read_att = flat_low(lax.psum(read_part, "blk"), query_rows)
    write_mix, write_lse = attend(write_query, write_keys, write_values, write_extra, factor)
    write_att = flat_low(write_mix, vis_rows)
    read_sum, write_sum = head_total(matmul(read_att, read_out), matmul(write_att, write_out))
    query_two = query_one + read_sum
    vis_two = vis_one + write_sum
    feed_vis_norm, feed_vis_hat, feed_vis_inv = layer_norm(vis_two, norm_gains[4])
    feed_vis_low = feed_vis_norm.astype(jnp.bfloat16)
    vis_hidden = matmul(feed_vis_low, vis_up)
    vis_act = exact_gelu(vis_hidden).astype(jnp.bfloat16)
    feed_query_norm, feed_query_hat, feed_query_inv = layer_norm(query_two, norm_gains[5])
    feed_query_low = feed_query_norm.astype(jnp.bfloat16)
    query_hidden = matmul(feed_query_low, query_up)
    query_act = exact_gelu(query_hidden).astype(jnp.bfloat16)
    vis_feed, query_feed = head_total(matmul(vis_act, vis_down), matmul(query_act, query_down))
    vis_three = vis_two + vis_feed
    query_three = query_two + query_feed
    grad_vis3 = cot_vis[0].astype(jnp.float32)
    grad_query3 = cot_query[0].astype(jnp.float32)
    vis_back, vis_up_grad, vis_down_grad = feed_back(
        grad_vis3, feed_vis_low, vis_hidden, vis_act, vis_up, vis_down, same
    )
    query_back, query_up_grad, query_down_grad = feed_back(
        grad_query3, feed_query_low, query_hidden, query_act, query_up, query_down, own
    )
    vis_back, query_back = head_total(vis_back, query_back)
    grad_vis2 = grad_vis3 + norm_back(vis_back, feed_vis_hat, feed_vis_inv, norm_gains[4])
    grad_query2 = grad_query3 + norm_back(query_back, feed_query_hat, feed_query_inv, norm_gains[5])
    gain_feed_vis = jnp.sum(vis_back * feed_vis_hat, axis=0)
    gain_feed_query = jnp.sum(own(query_back) * own(feed_query_hat), axis=0)
    vis2_low = grad_vis2.astype(jnp.bfloat16)
    query2_low = grad_query2.astype(jnp.bfloat16)
    read_out_grad = inner_rows(own(read_att), own(query2_low))
    write_out_grad = inner_rows(write_att, vis2_low)
    read_grad_att = split(times_back(query2_low, read_out).astype(jnp.bfloat16), 1)
    write_grad_att = split(times_back(vis2_low, write_out).astype(jnp.bfloat16), 1)
    write_dq, write_dk, write_dv, write_ds = attend_back(
        write_grad_att, write_query, write_keys, write_values, write_extra, write_lse, factor, same
    )

    def partial_rows(rowdot):
        return lax.psum(rowdot, "blk")

    read_dq, read_dk, read_dv, read_ds = attend_back(
        read_grad_att, read_query, read_keys, read_values, 0.0, read_lse, factor, partial_rows
    )
    read_dq, write_dk, write_dv = lax.psum((read_dq, write_dk, write_dv), "blk")
    read_dq_low = flat_low(read_dq, query_rows)
    read_dk_low = flat_low(read_dk, vis_rows)
    read_dv_low = flat_low(read_dv, vis_rows)
    write_dq_low = flat_low(write_dq, vis_rows)
    write_dk_low = flat_low(write_dk, query_rows)
    write_dv_low = flat_low(write_dv, query_rows)
    cross_query_back = (
        times_back(read_dq_low, read_qkv[0])
        + times_back(write_dk_low, write_qkv[1])
        + times_back(write_dv_low, write_qkv[2])
    )
    cross_vis_back = (
        times_back(read_dk_low, read_qkv[1])
        + times_back(read_dv_low, read_qkv[2])
        + times_back(write_dq_low, write_qkv[0])
    )
    read_qkv_grad = jnp.stack(
        [
            inner_rows(own(cross_query_low), own(read_dq_low)),
            inner_rows(cross_vis_low, read_dk_low),
            inner_rows(cross_vis_low, read_dv_low),
        ]
    )
    write_qkv_grad = jnp.stack(
        [
            inner_rows(cross_vis_low, write_dq_low),
            inner_rows(own(cross_query_low), own(write_dk_low)),
            inner_rows(own(cross_query_low), own(write_dv_low)),
        ]
    )
    cross_query_back, cross_vis_back = head_total(cross_query_back, cross_vis_back)
    grad_query1 = grad_query2 + norm_back(
        cross_query_back, cross_query_hat, cross_query_inv, norm_gains[2]
    )
    grad_vis1 = grad_vis2 + norm_back(cross_vis_back, cross_vis_hat, cross_vis_inv, norm_gains[3])
    gain_cross_query = jnp.sum(own(cross_query_back) * own(cross_query_hat), axis=0)
    gain_cross_vis = jnp.sum(cross_vis_back * cross_vis_hat, axis=0)
    vis1_low = grad_vis1.astype(jnp.bfloat16)
    query1_low = grad_query1.astype(jnp.bfloat16)
    window_out_grad = inner_rows(window_att, vis1_low)
    causal_out_grad = inner_rows(own(causal_att), own(query1_low))
    window_dq, window_dk, window_dv, window_ds = attend_back(
        split(times_back(vis1_low, window_out).astype(jnp.bfloat16), windows),
        window_query,
        window_keys,
        window_values,
        window_extra,
        window_lse,
        factor,
        same,
    )
    window_lows = [flat_low(tensor, vis_rows) for tensor in (window_dq, window_dk, window_dv)]
    window_qkv_grad = jnp.stack([inner_rows(window_low, member) for member in window_lows])
    window_back = (
        times_back(window_lows[0], window_qkv[0])
        + times_back(window_lows[1], window_qkv[1])
        + times_back(window_lows[2], window_qkv[2])
    )
    summed = jnp.sum(window_ds, axis=0).reshape(local_heads, WIN, WIN, WIN, WIN)
    table_grad = jnp.einsum("pqa,rsb,hprqs->hab", one_hot, one_hot, summed, precision=HIGH)
    causal_dq, causal_dk, causal_dv, causal_ds = attend_back(
        split(times_back(query1_low, causal_out).astype(jnp.bfloat16), 1),
        causal_query,
        causal_keys,
        causal_values,
        causal_extra,
        causal_lse,
        factor,
        same,
    )
    causal_lows = [flat_low(tensor, query_rows) for tensor in (causal_dq, causal_dk, causal_dv)]
    causal_qkv_grad = jnp.stack(
        [inner_rows(own(causal_low), own(member)) for member in causal_lows]
    )
    causal_back = (
        times_back(causal_lows[0], causal_qkv[0])
        + times_back(causal_lows[1], causal_qkv[1])
        + times_back(causal_lows[2], causal_qkv[2])
    )
    window_back, causal_back = head_total(window_back, causal_back)
    grad_vis0 = grad_vis1 + norm_back(window_back, window_hat, window_inv, norm_gains[0])
    grad_query0 = grad_query1 + norm_back(causal_back, causal_hat, causal_inv, norm_gains[1])
    gain_window = jnp.sum(window_back * window_hat, axis=0)
    gain_causal = jnp.sum(own(causal_back) * own(causal_hat), axis=0)
    gain_grad = jnp.stack(
        [gain_window, gain_causal, gain_cross_query, gain_cross_vis, gain_feed_vis, gain_feed_query]
    )
    (
        gains_part,
        window_qkv_part,
        window_out_part,
        causal_qkv_part,
        causal_out_part,
        read_qkv_part,
        read_out_part,
        write_qkv_part,
        write_out_part,
        vis_up_part,
        vis_down_part,
        query_up_part,
        query_down_part,
    ) = (
        lax.psum_scatter(gain_grad, ("page", "blk"), scatter_dimension=1, tiled=True),
        lax.psum_scatter(window_qkv_grad, ("page", "blk"), scatter_dimension=1, tiled=True),
        lax.psum_scatter(window_out_grad, ("page", "blk"), scatter_dimension=1, tiled=True),
        lax.psum_scatter(causal_qkv_grad, ("page", "blk"), scatter_dimension=1, tiled=True),
        lax.psum_scatter(causal_out_grad, ("page", "blk"), scatter_dimension=1, tiled=True),
        lax.psum_scatter(read_qkv_grad, ("page", "blk"), scatter_dimension=1, tiled=True),
        lax.psum_scatter(read_out_grad, ("page", "blk"), scatter_dimension=1, tiled=True),
        lax.psum_scatter(write_qkv_grad, ("page", "blk"), scatter_dimension=1, tiled=True),
        lax.psum_scatter(write_out_grad, ("page", "blk"), scatter_dimension=1, tiled=True),
        lax.psum_scatter(vis_up_grad, ("page", "blk"), scatter_dimension=0, tiled=True),
        lax.psum_scatter(vis_down_grad, ("page", "blk"), scatter_dimension=1, tiled=True),
        lax.psum_scatter(query_up_grad, ("page", "blk"), scatter_dimension=0, tiled=True),
        lax.psum_scatter(query_down_grad, ("page", "blk"), scatter_dimension=1, tiled=True),
    )
    table_part = lax.psum(table_grad, ("page", "blk"))
    return (
        vis_three.astype(jnp.bfloat16)[None],
        query_three.astype(jnp.bfloat16)[None],
        grad_vis0[None],
        grad_query0[None],
        gains_part,
        table_part,
        window_qkv_part,
        window_out_part,
        causal_qkv_part,
        causal_out_part,
        read_qkv_part,
        read_out_part,
        write_qkv_part,
        write_out_part,
        vis_up_part,
        vis_down_part,
        query_up_part,
        query_down_part,
    )


def fits(mesh, args):
    nb = mesh.shape["blk"]
    rows, width = args[0].shape[1:]
    queries = args[1].shape[1]
    heads = args[4].shape[0]
    return (
        nb % 2 == 0
        and mesh.shape["page"] == 2
        and mesh.shape["head"] == 2
        and rows == AREA * nb
        and queries % (16 * nb) == 0
        and width % (32 * nb) == 0
        and heads % 4 == 0
        and heads <= 16
    )


def solution(mesh):
    in_specs = (
        P("page", "blk", None),
        P("page", None, None),
        P("page"),
        P(),
        P("head", None, None),
        P(None, None, "head"),
        P("head", None),
        P(None, None, "head"),
        P("head", None),
        P(None, None, "head"),
        P("head", None),
        P(None, None, "head"),
        P("head", None),
        P(None, "head"),
        P("head", None),
        P(None, "head"),
        P("head", None),
        P("page", "blk", None),
        P("page", None, None),
    )
    out_specs = (
        P("page", "blk", None),
        P("page", None, None),
        P("page", "blk", None),
        P("page", None, None),
        P(None, ("page", "blk")),
        P("head", None, None),
        P(None, ("page", "blk"), "head"),
        P("head", ("page", "blk")),
        P(None, ("page", "blk"), "head"),
        P("head", ("page", "blk")),
        P(None, ("page", "blk"), "head"),
        P("head", ("page", "blk")),
        P(None, ("page", "blk"), "head"),
        P("head", ("page", "blk")),
        P(("page", "blk"), "head"),
        P("head", ("page", "blk")),
        P(("page", "blk"), "head"),
        P("head", ("page", "blk")),
    )

    def step(*args):
        body = fused_shards if fits(mesh, args) else shards
        return jax.shard_map(body, mesh=mesh, in_specs=in_specs, out_specs=out_specs, check_vma=False)(*args)

    return step
```
